256 devices in a mesh: replica: 64 (over z_hi, y, x), fsdp: 4 (over z_lo, core).
Axes of the slice: x: 4, y: 4, z: 8 (z_hi: 4, z_lo: 2; z = z_hi * 2 + z_lo), core: 2. Of those that a mesh axis runs over, the one named last changes fastest.
Arguments:
- inputs: bfloat16 [32768, 2048], P(('replica', 'fsdp')), may hold values from -6 to 6
- weights: bfloat16 [131072, 4608], P('replica', 'fsdp'), may hold values from -1.155 to 1.155
- cotangent: bfloat16 [32768, 4608], P('replica', 'fsdp'), may hold values from -6 to 6
- gain: float32 [4608], P('fsdp'), may hold values from -0.5 to 1
- snapshot: bfloat16 [8192, 4608], P('replica', 'fsdp'), may hold values from -3 to 3
- global_rows: float32 [128, 4608], P(None, 'fsdp'), may hold values from -3 to 3
- momentum: float32 [128, 4608], P(None, 'fsdp'), may hold values from -3 to 3
- plan: int32 [16], replicated, may hold values from 0 to 15, as said below
- delay: int32 [1], replicated, may hold values from 1 to 15
Outputs:
- new_weights: bfloat16 [131072, 4608], P('replica', 'fsdp')
- new_global: float32 [128, 4608], P(None, 'fsdp')
- new_momentum: float32 [128, 4608], P(None, 'fsdp')
The draws below stay inside these ranges and needn't reach their ends.
Inputs may be any that keep to these rules, and one draw needn't show every extreme that they name: `plan`: the 16 entries are distinct fragment ids.
All inputs are finite; a program needn't handle non-finite values.
Results may differ from the reference program's by a relative error of at most 0.0042.
Values may be sent and summed in bfloat16 or wider, within the bound.
A program may use at most 128 MiB of HBM per device.

```python
import math
import jax
import jax.numpy as jnp
from jax import lax

D = 4608
HD = 2048
TOKENS_REP = 512
REPLICAS = 64
FRAG_ROWS = 128
FRAGS = 16
SCHED = 16


def draw_weights(key, part):
    key = jax.random.fold_in(key, 11)
    key_base, key_cols = jax.random.split(key)
    columns = jnp.arange(D, dtype=jnp.float32) / max(D - 1, 1)
    base = jax.random.truncated_normal(key_base, -4.0, 4.0, (REPLICAS * HD, D), jnp.float32)
    ramp = 1.0 + 2.0 * columns
    spread = jnp.exp(jax.random.uniform(key_cols, (D,), jnp.float32, 0.0, math.log(4.0)))
    return (base * (ramp * spread)[None, :] / 48.0).astype(jnp.bfloat16)


def draw_plan(key, part):
    key = jax.random.fold_in(key, 23)
    order = jax.random.permutation(key, FRAGS)
    return order[:SCHED].astype(jnp.int32)


def block_scale(rng, shape, shards, low, high):
    level, own = 1.0, jax.random.fold_in(rng, 6)
    for dim, blocks in shards:
        draws = jnp.exp(jax.random.uniform(jax.random.fold_in(own, dim), (blocks,), jnp.float32, low / len(shards), high / len(shards)))
        level = level * jnp.repeat(draws, shape[dim] // blocks).reshape([-1 if axis == dim else 1 for axis in range(len(shape))])
    return level


def scatter_about(key, dims, deviation, reach, cuts=(), kind=jnp.bfloat16):
    result = jax.random.normal(key, dims, jnp.float32) * deviation
    if len(cuts) > 0:
        result = block_scale(key, dims, cuts, -0.22, 0.18) * result
    return jnp.clip(result, min=-reach, max=reach).astype(kind)


def setup_inputs(seed: int = 0) -> dict:
    key_of = jax.random.split(jax.random.key(seed), 10)
    return {
        "inputs": scatter_about(key_of[0], (REPLICAS * TOKENS_REP, HD), 1.0, 6.0, ((0, 256),)),
        "weights": draw_weights(jax.random.fold_in(key_of[9], 71), 0),
        "cotangent": scatter_about(key_of[2], (REPLICAS * TOKENS_REP, D), 1.0, 6.0, ((0, 64), (1, 4))),
        "gain": jnp.clip(-0.5 + 1.5 * jax.random.uniform(key_of[3], (D,), jnp.float32) ** block_scale(key_of[3], (D,), ((0, 4),), -0.2, 0.2), -0.5, 1.0),
        "snapshot": scatter_about(key_of[4], (REPLICAS * FRAG_ROWS, D), 0.2, 3.0, ((0, 64), (1, 4))),
        "global_rows": scatter_about(key_of[5], (FRAG_ROWS, D), 0.2, 3.0, ((1, 4),), jnp.float32),
        "momentum": scatter_about(key_of[6], (FRAG_ROWS, D), 0.2, 3.0, ((1, 4),), jnp.float32),
        "plan": draw_plan(jax.random.fold_in(key_of[9], 71), 0),
        "delay": jax.random.randint(key_of[8], (1,), 1, SCHED).astype(jnp.int32),
    }


norm_eps = 1e-06
inner_rate = 0.02
outer_rate = 0.7
outer_beta = 0.9
merge_weight = 0.5

def reference(inputs, weights, cotangent, gain, snapshot, global_rows, momentum, plan, delay):
    snaps = snapshot.reshape(REPLICAS, FRAG_ROWS, D).astype(jnp.float32)
    outer_grad = lax.optimization_barrier(jnp.sum(global_rows[None] - snaps, axis=0)) / REPLICAS
    new_momentum = outer_beta * momentum + outer_grad
    new_global = global_rows - outer_rate * (outer_grad + outer_beta * new_momentum)
    position = (SCHED - 1 - delay[0]).astype(jnp.int32)
    fragment = lax.dynamic_index_in_dim(plan, position, 0, keepdims=False)
    first_row = (fragment * FRAG_ROWS).astype(jnp.int32)
    gain_factor = 1.0 + gain

    def one_replica(packed):
        tokens, weight_block, cot_block = packed
        proj = jnp.dot(tokens, weight_block, preferred_element_type=jnp.float32)
        inverse = lax.rsqrt(lax.optimization_barrier(jnp.sum(proj * proj, axis=1)) / D + norm_eps)
        scaled = cot_block.astype(jnp.float32) * gain_factor[None, :]
        project_dot = lax.optimization_barrier(jnp.sum(scaled * proj, axis=1)) / D
        dproj = (inverse[:, None] * scaled - proj * (inverse ** 3 * project_dot)[:, None]).astype(jnp.bfloat16)
        grad = jnp.dot(tokens.T, dproj, preferred_element_type=jnp.float32)
        stepped = weight_block.astype(jnp.float32) - inner_rate * grad
        chosen = lax.dynamic_slice_in_dim(stepped, first_row, FRAG_ROWS, 0)
        mixed = (1.0 - merge_weight) * chosen + merge_weight * new_global
        merged = lax.dynamic_update_slice_in_dim(stepped, mixed, first_row, 0)
        return merged.astype(jnp.bfloat16)
    blocks = lax.map(one_replica, (inputs.reshape(REPLICAS, TOKENS_REP, HD), weights.reshape(REPLICAS, HD, D), cotangent.reshape(REPLICAS, TOKENS_REP, D)))
    return (blocks.reshape(REPLICAS * HD, D), new_global, new_momentum)
```

```python
import functools

import jax
import jax.numpy as jnp
from jax import lax
from jax.experimental import pallas as pl
from jax.experimental.pallas import tpu as pltpu
from jax.sharding import PartitionSpec as P

norm_eps = 1e-06
inner_rate = 0.02
outer_rate = 0.7
outer_beta = 0.9
merge_weight = 0.5

GRID = (4, 4, 4)
CHUNKS = 4

f32 = jnp.float32
bf16 = jnp.bfloat16


def split_columns(width):
    first = (width // 128 + 1) // 2 * 128
    return ((0, first), (first, width))


def exchange_kernel(
    x_hbm, w_hbm, cot_hbm, gain_ref, snap_hbm, global_hbm, momentum_hbm,
    w_ref, xt_ref, dproj_ref, new_global_ref, new_momentum_ref,
    xbuf, cot, proj, message, sums, total, old_global, old_momentum,
    snap_a, snap_b, part_a, part_b, have_a, have_b, plane_a, plane_b,
    local_sem, sib_send, sib_recv, far_send, far_recv, fwd_send, fwd_recv,
    sum_send, sum_recv, outer_send, outer_recv,
):
    nz, ny, nx = GRID
    replicas = nz * ny * nx
    r = lax.axis_index("replica")
    f = lax.axis_index("fsdp")
    x = lax.rem(r, nx)
    y = lax.rem(lax.div(r, nx), ny)
    z = lax.div(r, nx * ny)
    core = lax.rem(f, 2)
    sibling = f + 1 - 2 * core
    far = lax.rem(f + 2, 4)
    far_sibling = 3 - f
    _, chunks, step, _ = xbuf.shape
    rows = 4 * step
    width = w_ref.shape[1]
    model = 4 * width

    def x_peer(d):
        return {"replica": r - x + lax.rem(x + d, nx)}

    def y_peer(d):
        return {"replica": r + nx * (lax.rem(y + d, ny) - y)}

    def z_peer(d):
        return {"replica": r + nx * ny * (lax.rem(z + d, nz) - z)}

    def fsdp_peer(which):
        return {"fsdp": which}

    sent = []

    def remote(src, dst, send, recv, where):
        copy = pltpu.make_async_remote_copy(
            src_ref=src, dst_ref=dst, send_sem=send, recv_sem=recv,
            device_id=where, device_id_type=pl.DeviceIdType.MESH,
        )
        sent.append(copy)
        return copy

    cut_a, cut_b = split_columns(width)
    halves = (
        (cut_a, (x, nx, x_peer), (y, ny, y_peer), snap_a, part_a, have_a, plane_a),
        (cut_b, (y, ny, y_peer), (x, nx, x_peer), snap_b, part_b, have_b, plane_b),
    )
    height = total.shape[0]

    mine = [
        pltpu.make_async_copy(x_hbm, xbuf.at[f], local_sem.at[0]),
        pltpu.make_async_copy(w_hbm, w_ref, local_sem.at[1]),
        pltpu.make_async_copy(cot_hbm, cot, local_sem.at[2]),
        pltpu.make_async_copy(global_hbm, old_global, local_sem.at[3]),
        pltpu.make_async_copy(momentum_hbm, old_momentum, local_sem.at[4]),
    ]
    own_snap = []
    for h, ((lo, hi), (i, n, _), _, snaps, _, _, _) in enumerate(halves):
        block = height // n
        own_snap.append(
            pltpu.make_async_copy(
                snap_hbm.at[pl.ds(i * block, block), pl.ds(lo, hi - lo)],
                snaps.at[n - 1],
                local_sem.at[5 + h],
            )
        )

    barrier = pltpu.get_barrier_semaphore()
    partners = [fsdp_peer(sibling), fsdp_peer(far), fsdp_peer(far_sibling)]
    partners += [x_peer(d) for d in range(1, nx)]
    partners += [y_peer(d) for d in range(1, ny)]
    partners += [z_peer(d) for d in range(1, nz)]
    for where in partners:
        pl.semaphore_signal(barrier, inc=1, device_id=where, device_id_type=pl.DeviceIdType.MESH)
    for copy in mine + own_snap:
        copy.start()
    pl.semaphore_wait(barrier, len(partners))

    far_copy, sib_copy, fwd_copy = [], [], []
    for c in range(chunks):
        far_copy.append(
            remote(x_hbm.at[c], xbuf.at[f, c], far_send.at[c], far_recv.at[c], fsdp_peer(far))
        )
        sib_copy.append(
            remote(x_hbm.at[c], xbuf.at[f, c], sib_send.at[c], sib_recv.at[c], fsdp_peer(sibling))
        )
        far_copy[c].start()
        sib_copy[c].start()

    def scatter_first(h):
        (lo, hi), (i, n, peer), _, snaps, _, _, _ = halves[h]
        block = height // n
        copies = []
        for d in range(1, n):
            there = lax.rem(i + d, n)
            copies.append(
                remote(
                    snap_hbm.at[pl.ds(there * block, block), pl.ds(lo, hi - lo)],
                    snaps.at[d - 1],
                    outer_send.at[0, h, d - 1], outer_recv.at[0, h, d - 1], peer(d),
                )
            )
        for copy in copies:
            copy.start()
        return copies

    def scatter_second(h, before):
        _, (_, n, _), (j, m, peer), snaps, part, have, _ = halves[h]
        for copy in before:
            copy.wait_recv()
        own_snap[h].wait()
        amount = snaps[0].astype(f32)
        for k in range(1, n):
            amount += snaps[k].astype(f32)
        part[...] = amount
        size = part.shape[0] // m
        copies = []
        for d in range(1, m):
            there = lax.rem(j + d, m)
            copies.append(
                remote(
                    part.at[pl.ds(there * size, size)], have.at[d - 1],
                    outer_send.at[1, h, d - 1], outer_recv.at[1, h, d - 1], peer(d),
                )
            )
        for copy in copies:
            copy.start()
        return copies

    def across_planes(h, before):
        _, _, (j, m, _), _, part, have, plane = halves[h]
        for copy in before:
            copy.wait_recv()
        size = part.shape[0] // m
        amount = part[pl.ds(pl.multiple_of(j * size, size), size), :]
        for k in range(m - 1):
            amount += have[k]
        plane[z] = amount
        copies = []
        for d in range(1, nz):
            copies.append(
                remote(
                    plane.at[z], plane.at[z],
                    outer_send.at[2, h, d - 1], outer_recv.at[2, h, d - 1], z_peer(d),
                )
            )
        for copy in copies:
            copy.start()
        return copies

    def gather_second(h, before):
        (lo, hi), (i, n, _), (j, m, peer), _, _, _, plane = halves[h]
        for copy in before:
            copy.wait_recv()
        amount = plane[0]
        for k in range(1, nz):
            amount += plane[k]
        size = height // (n * m)
        here = pl.ds(pl.multiple_of((i * m + j) * size, size), size)
        total[here, lo:hi] = amount
        copies = []
        for d in range(1, m):
            place = total.at[here, pl.ds(lo, hi - lo)]
            copies.append(
                remote(place, place, outer_send.at[3, h, d - 1], outer_recv.at[3, h, d - 1], peer(d))
            )
        for copy in copies:
            copy.start()
        return copies

    def gather_first(h, before):
        (lo, hi), (i, n, peer), _, _, _, _, _ = halves[h]
        for copy in before:
            copy.wait_recv()
        block = height // n
        copies = []
        for d in range(1, n):
            place = total.at[pl.ds(i * block, block), pl.ds(lo, hi - lo)]
            copies.append(
                remote(place, place, outer_send.at[4, h, d - 1], outer_recv.at[4, h, d - 1], peer(d))
            )
        for copy in copies:
            copy.start()
        return copies

    stages = (scatter_second, across_planes, gather_second, gather_first)
    outer = [scatter_first(h) for h in range(2)]
    gain_factor = 1.0 + gain_ref[...]

    def scaled_of(c):
        return cot[:, c].reshape(rows, width).astype(f32) * gain_factor

    def lanes(value):
        amount = value[:, :128]
        for k in range(128, width, 128):
            amount += value[:, k : k + 128]
        return jnp.sum(amount.T, axis=0, keepdims=True)

    def project(c):
        tokens = xbuf[:, c].reshape(rows, xbuf.shape[3])
        value = jnp.dot(tokens, w_ref[...], preferred_element_type=f32)
        proj[c] = value
        message[c, 0:1, :] = lanes(value * value)
        message[c, 1:2, :] = lanes(scaled_of(c) * value)
        copies = []
        for d, where in enumerate((sibling, far, far_sibling)):
            copies.append(
                remote(
                    message.at[c], sums.at[c, d],
                    sum_send.at[c, d], sum_recv.at[c, d], fsdp_peer(where),
                )
            )
        for copy in copies:
            copy.start()
        xt_ref[:, c * rows : (c + 1) * rows] = tokens.T
        return copies

    def column(value):
        return jnp.broadcast_to(value, (128, rows)).T

    def finish(c, before):
        for copy in before:
            copy.wait_recv()
        both = message[c] + sums[c, 0] + sums[c, 1] + sums[c, 2]
        inverse = lax.rsqrt(both[0:1] / model + norm_eps)
        factor = inverse * inverse * inverse * (both[1:2] / model)
        inverse, factor = column(inverse), column(factor)
        scaled = scaled_of(c)
        for k in range(0, width, 128):
            value = inverse * scaled[:, k : k + 128] - proj[c, :, k : k + 128] * factor
            dproj_ref[c * rows : (c + 1) * rows, k : k + 128] = value.astype(bf16)

    message[...] = jnp.zeros_like(message)
    pending = None
    for c in range(chunks):
        far_copy[c].wait_recv()
        fwd_copy.append(
            remote(
                xbuf.at[far, c], xbuf.at[far, c], fwd_send.at[c], fwd_recv.at[c], fsdp_peer(sibling)
            )
        )
        fwd_copy[c].start()
        outer = [stages[c](h, outer[h]) for h in range(2)]
        if c == 0:
            for copy in mine[:3]:
                copy.wait()
        sib_copy[c].wait_recv()
        fwd_copy[c].wait_recv()
        now = project(c)
        if pending is not None:
            finish(c - 1, pending)
        pending = now
    finish(chunks - 1, pending)
    for h in range(2):
        for copy in outer[h]:
            copy.wait_recv()
    for copy in mine[3:]:
        copy.wait()
    outer_grad = old_global[...] - total[...] / replicas
    new_momentum = outer_beta * old_momentum[...] + outer_grad
    new_momentum_ref[...] = new_momentum
    new_global_ref[...] = old_global[...] - outer_rate * (outer_grad + outer_beta * new_momentum)
    for copy in sent:
        copy.wait_send()


def update_kernel(
    plan_ref, delay_ref, w_ref, xt_ref, dproj_ref, new_global_ref, new_momentum_ref,
    out_hbm, global_hbm, momentum_hbm, tile, tile_sem, outer_sem,
):
    slots, step, _ = tile.shape
    height = new_global_ref.shape[0]
    steps = w_ref.shape[0] // step
    fragment = plan_ref[plan_ref.shape[0] - 1 - delay_ref[0]]
    outer = [
        pltpu.make_async_copy(new_global_ref, global_hbm, outer_sem.at[0]),
        pltpu.make_async_copy(new_momentum_ref, momentum_hbm, outer_sem.at[1]),
    ]
    for copy in outer:
        copy.start()
    copies = []
    for i in range(steps):
        slot = i % slots
        if i >= slots:
            copies[i - slots].wait()
        here = slice(i * step, (i + 1) * step)
        grad = jnp.dot(xt_ref[here], dproj_ref[...], preferred_element_type=f32)
        stepped = w_ref[here].astype(f32) - inner_rate * grad
        tile[slot] = stepped.astype(bf16)
        for k in range(step // height):

            @pl.when(fragment == i * (step // height) + k)
            def _():
                part = slice(k * height, (k + 1) * height)
                chosen = stepped[part]
                mixed = (1.0 - merge_weight) * chosen + merge_weight * new_global_ref[...]
                tile[slot, part] = mixed.astype(bf16)

        copies.append(
            pltpu.make_async_copy(tile.at[slot], out_hbm.at[pl.ds(i * step, step)], tile_sem.at[slot])
        )
        copies[i].start()
    for copy in copies[max(steps - slots, 0) :] + outer:
        copy.wait()


def local(inputs, weights, cotangent, gain, snapshot, global_rows, momentum, plan, delay):
    tokens, features = inputs.shape
    width = weights.shape[1]
    height = snapshot.shape[0]
    chunks = CHUNKS
    step = tokens // chunks
    nz, ny, nx = GRID
    cut_a, cut_b = split_columns(width)
    wide_a, wide_b = cut_a[1] - cut_a[0], cut_b[1] - cut_b[0]
    size = height // (nx * ny)
    most = max(nx, ny, nz)
    hbm = pl.BlockSpec(memory_space=pltpu.HBM)
    vmem = pl.BlockSpec(memory_space=pltpu.VMEM)
    smem = pl.BlockSpec(memory_space=pltpu.SMEM)
    dma = pltpu.SemaphoreType.DMA
    kept = pl.pallas_call(
        exchange_kernel,
        name="exchange",
        out_shape=(
            pltpu.VMEM((features, width), bf16),
            pltpu.VMEM((features, 4 * tokens), bf16),
            pltpu.VMEM((4 * tokens, width), bf16),
            pltpu.VMEM((height, width), f32),
            pltpu.VMEM((height, width), f32),
        ),
        in_specs=[hbm, hbm, hbm, vmem, hbm, hbm, hbm],
        out_specs=(vmem,) * 5,
        scratch_shapes=[
            pltpu.VMEM((4, chunks, step, features), bf16),
            pltpu.VMEM((4, chunks, step, width), bf16),
            pltpu.VMEM((chunks, 4 * step, width), f32),
            pltpu.VMEM((chunks, 8, 4 * step), f32),
            pltpu.VMEM((chunks, 3, 8, 4 * step), f32),
            pltpu.VMEM((height, width), f32),
            pltpu.VMEM((height, width), f32),
            pltpu.VMEM((height, width), f32),
            pltpu.VMEM((nx, height // nx, wide_a), bf16),
            pltpu.VMEM((ny, height // ny, wide_b), bf16),
            pltpu.VMEM((height // nx, wide_a), f32),
            pltpu.VMEM((height // ny, wide_b), f32),
            pltpu.VMEM((ny - 1, size, wide_a), f32),
            pltpu.VMEM((nx - 1, size, wide_b), f32),
            pltpu.VMEM((nz, size, wide_a), f32),
            pltpu.VMEM((nz, size, wide_b), f32),
            dma((7,)),
            dma((chunks,)),
            dma((chunks,)),
            dma((chunks,)),
            dma((chunks,)),
            dma((chunks,)),
            dma((chunks,)),
            dma((chunks, 3)),
            dma((chunks, 3)),
            dma((5, 2, most - 1)),
            dma((5, 2, most - 1)),
        ],
        compiler_params=pltpu.CompilerParams(
            collective_id=0, has_side_effects=True, vmem_limit_bytes=32 * 2**20
        ),
    )(
        inputs.reshape(chunks, step, features),
        weights,
        cotangent.reshape(4, chunks, step, width),
        gain.reshape(1, width),
        snapshot,
        global_rows,
        momentum,
    )
    kept = [pltpu.with_memory_space_constraint(value, pltpu.VMEM) for value in kept]
    block = 256 if features % 256 == 0 else 128
    return pl.pallas_call(
        update_kernel,
        name="update",
        out_shape=(
            jax.ShapeDtypeStruct((features, width), bf16),
            jax.ShapeDtypeStruct((height, width), f32),
            jax.ShapeDtypeStruct((height, width), f32),
        ),
        in_specs=[smem, smem] + [vmem] * 5,
        out_specs=(hbm,) * 3,
        scratch_shapes=[
            pltpu.VMEM((4, block, width), bf16),
            dma((4,)),
            dma((2,)),
        ],
        compiler_params=pltpu.CompilerParams(vmem_limit_bytes=24 * 2**20),
    )(plan, delay, *kept)


def solution(mesh):
    in_specs = (
        P(("replica", "fsdp"), None),
        P("replica", "fsdp"),
        P("replica", "fsdp"),
        P("fsdp"),
        P("replica", "fsdp"),
        P(None, "fsdp"),
        P(None, "fsdp"),
        P(),
        P(),
    )
    out_specs = (P("replica", "fsdp"), P(None, "fsdp"), P(None, "fsdp"))
    return jax.shard_map(local, mesh=mesh, in_specs=in_specs, out_specs=out_specs, check_vma=False)
```

```python
import functools

import jax
import jax.numpy as jnp
from jax import lax
from jax.experimental import pallas as pl
from jax.experimental.pallas import tpu as pltpu
from jax.sharding import PartitionSpec as P

norm_eps = 1e-06
inner_rate = 0.02
outer_rate = 0.7
outer_beta = 0.9
merge_weight = 0.5

GRID = (4, 4, 4)
CHUNKS = 4
AHEAD = 2

f32 = jnp.float32
bf16 = jnp.bfloat16


def split_columns(width):
    first = (width // 128 + 1) // 2 * 128
    return ((0, first), (first, width))


def exchange_kernel(
    x_hbm, w_hbm, cot_hbm, gain_hbm, snap_hbm, global_hbm, momentum_hbm,
    x_ref, w_ref, dproj, stepped_ref, total, old_global, old_momentum,
    cot, gain, proj, grad, message, sums,
    snaps, plane,
    local_sem, sib_send, sib_recv, far_send, far_recv, fwd_send, fwd_recv,
    sum_send, sum_recv, scatter_send, scatter_recv, plane_send, plane_recv,
    axis_send, axis_recv, gather_send, gather_recv,
):
    nz, ny, nx = GRID
    r = lax.axis_index("replica")
    f = lax.axis_index("fsdp")
    x = lax.rem(r, nx)
    y = lax.rem(lax.div(r, nx), ny)
    z = lax.div(r, nx * ny)
    place = lax.rem(r, nx * ny)
    core = lax.rem(f, 2)
    sibling = f + 1 - 2 * core
    far = lax.rem(f + 2, 4)
    far_sibling = 3 - f
    _, chunks, step, features = x_ref.shape
    rows = 4 * step
    width = w_ref.shape[1]
    model = 4 * width
    height = total.shape[0]
    size = height // (nx * ny)
    columns = split_columns(width)

    def x_peer(d):
        return {"replica": r - x + lax.rem(x + d, nx)}

    def y_peer(d):
        return {"replica": r + nx * (lax.rem(y + d, ny) - y)}

    def plane_peer(d):
        return {"replica": r - place + lax.rem(place + d, nx * ny)}

    def z_peer(d):
        return {"replica": r + nx * ny * (lax.rem(z + d, nz) - z)}

    def fsdp_peer(which):
        return {"fsdp": which}

    sent = []

    def send(src, dst, send_sem, recv_sem, where):
        copy = pltpu.make_async_remote_copy(
            src_ref=src, dst_ref=dst, send_sem=send_sem, recv_sem=recv_sem,
            device_id=where, device_id_type=pl.DeviceIdType.MESH,
        )
        copy.start()
        sent.append(copy)
        return copy

    barrier = pltpu.get_barrier_semaphore()
    partners = [fsdp_peer(sibling), fsdp_peer(far), fsdp_peer(far_sibling)]
    partners += [plane_peer(d) for d in range(1, nx * ny)]
    partners += [z_peer(d) for d in range(1, nz)]
    for where in partners:
        pl.semaphore_signal(barrier, inc=1, device_id=where, device_id_type=pl.DeviceIdType.MESH)

    mine = []
    for which, (src, dst) in enumerate((
        (w_hbm, w_ref), (x_hbm, x_ref.at[f]), (cot_hbm, cot), (gain_hbm, gain),
        (global_hbm, old_global), (momentum_hbm, old_momentum),
    )):
        mine.append(pltpu.make_async_copy(src, dst, local_sem.at[which]))
    mine.append(pltpu.make_async_copy(snap_hbm.at[place], snaps.at[0], local_sem.at[len(mine)]))
    mine[0].start()
    pl.semaphore_wait(barrier, len(partners))

    def scatter():
        return [
            send(
                snap_hbm.at[lax.rem(place + d, nx * ny)], snaps.at[d],
                scatter_send.at[d - 1], scatter_recv.at[d - 1], plane_peer(d),
            )
            for d in range(1, nx * ny)
        ]

    def across_planes(before):
        mine[-1].wait()
        for copy in before:
            copy.wait_recv()
        amount = snaps[0].astype(f32)
        for k in range(1, nx * ny):
            amount += snaps[k].astype(f32)
        plane[z] = amount
        return [
            send(plane.at[z], plane.at[z], plane_send.at[d - 1], plane_recv.at[d - 1], z_peer(d))
            for d in range(1, nz)
        ]

    def piece(k):
        return total.at[pl.ds(pl.multiple_of(k * size, size), size)]

    axes = ((nx, x_peer), (ny, y_peer))

    def gather_axes(before):
        for copy in before:
            copy.wait_recv()
        amount = plane[0]
        for k in range(1, nz):
            amount += plane[k]
        here = piece(place)
        here[...] = amount
        return [
            [
                send(here, here, axis_send.at[a, d - 1], axis_recv.at[a, d - 1], peer(d))
                for d in range(1, n)
            ]
            for a, (n, peer) in enumerate(axes)
        ]

    def gather_rest(before):
        arriving = []
        most = max(nx, ny)
        for d in sorted(range(1, most), key=lambda d: min(d, most - d)):
            for a, (n, _) in enumerate(axes):
                if d >= n:
                    continue
                before[a][d - 1].wait_recv()
                from_x = place - x + lax.rem(x + nx - d, nx)
                from_y = place + nx * (lax.rem(y + ny - d, ny) - y)
                lo, hi = columns[1 - a]
                part = piece((from_x, from_y)[a]).at[:, pl.ds(lo, hi - lo)]
                m, peer = axes[1 - a]
                for e in range(1, m):
                    arriving.append(
                        send(
                            part, part,
                            gather_send.at[a, d - 1, e - 1], gather_recv.at[a, d - 1, e - 1], peer(e),
                        )
                    )
        return arriving

    def scaled_of(c):
        return cot[:, c].reshape(rows, width).astype(f32) * (1.0 + gain[...].reshape(1, width))

    def lanes(value):
        amount = value[:, :128]
        for k in range(128, width, 128):
            amount += value[:, k : k + 128]
        return jnp.sum(amount.T, axis=0, keepdims=True)

    def project(c):
        tokens = x_ref[:, c].reshape(rows, features)
        value = jnp.dot(tokens, w_ref[...], preferred_element_type=f32)
        proj[c] = value
        message[c, 0:1, :] = lanes(value * value)
        message[c, 1:2, :] = lanes(scaled_of(c) * value)
        return [
            send(
                message.at[c], sums.at[c, d], sum_send.at[c, d], sum_recv.at[c, d], fsdp_peer(where)
            )
            for d, where in enumerate((sibling, far, far_sibling))
        ]

    def column(value):
        return jnp.broadcast_to(value, (128, rows)).T

    def finish(c, before):
        for copy in before:
            copy.wait_recv()
        both = message[c] + sums[c, 0] + sums[c, 1] + sums[c, 2]
        inverse = lax.rsqrt(both[0:1] / model + norm_eps)
        factor = inverse * inverse * inverse * (both[1:2] / model)
        inverse, factor = column(inverse), column(factor)
        scaled = scaled_of(c)
        for k in range(0, width, 128):
            value = inverse * scaled[:, k : k + 128] - proj[c, :, k : k + 128] * factor
            dproj[:, c, :, k : k + 128] = value.astype(bf16).reshape(4, step, 128)

    def gradient(first, last, final):
        count = last - first
        right = dproj[:, first:last].reshape(count * rows, width)
        tile = min(256, features)
        for k in range(0, features, tile):
            left = x_ref[:, first:last, :, k : k + tile].reshape(count * rows, tile)
            value = lax.dot_general(
                left, right, (((0,), (0,)), ((), ())), preferred_element_type=f32
            )
            if final:
                value = w_ref[k : k + tile].astype(f32) - inner_rate * (grad[k : k + tile] + value)
                stepped_ref[k : k + tile] = value.astype(bf16)
            else:
                grad[k : k + tile] = value

    def x_part(c, sems, where):
        return send(x_hbm.at[c], x_ref.at[f, c], sems[0].at[c], sems[1].at[c], fsdp_peer(where))

    scattered = scatter()
    far_copy = [x_part(c, (far_send, far_recv), far) for c in range(min(AHEAD, chunks))]
    for copy in mine[1:]:
        copy.start()
    sib_copy = [x_part(c, (sib_send, sib_recv), sibling) for c in range(chunks)]
    message[...] = jnp.zeros_like(message)

    def forward(c):
        far_copy[c].wait_recv()
        if len(far_copy) < chunks:
            far_copy.append(x_part(len(far_copy), (far_send, far_recv), far))
        part = x_ref.at[far, c]
        return send(part, part, fwd_send.at[c], fwd_recv.at[c], fsdp_peer(sibling))

    def wave(c, copy):
        sib_copy[c].wait_recv()
        copy.wait_recv()
        return project(c)

    copy = forward(0)
    planes = across_planes(scattered)
    for local_copy in mine[:4]:
        local_copy.wait()
    half, last = chunks // 2, chunks - 1
    summing = [wave(0, copy)]
    for c in range(1, last):
        copy = forward(c)
        if c == last - 1:
            pieces = gather_axes(planes)
        summing.append(wave(c, copy))
        finish(c - 1, summing[c - 1])
    copy = forward(last)
    summing.append(wave(last, copy))
    arriving = gather_rest(pieces)
    gradient(0, half, False)
    finish(last - 1, summing[last - 1])
    finish(last, summing[last])
    gradient(half, chunks, True)
    for local_copy in mine[4:-1]:
        local_copy.wait()
    for copy in arriving:
        copy.wait_recv()
    for copy in sent:
        copy.wait_send()


def update_kernel(
    plan_ref, delay_ref, x_ref, w_ref, dproj, stepped_ref, total, old_global, old_momentum,
    out_hbm, global_hbm, momentum_hbm, new_global, new_momentum, merged, block_sem, last_sem,
):
    height, width = total.shape
    tokens = x_ref.shape[0] * x_ref.shape[1] * x_ref.shape[2]
    plan = plan_ref[...].reshape(1, plan_ref.shape[0])
    position = plan.shape[1] - 1 - delay_ref[...].reshape(1, 1)
    chosen = lax.broadcasted_iota(jnp.int32, plan.shape, 1) == position
    fragment = jnp.sum(jnp.where(chosen, plan, 0))
    blocks = []
    for k in range(w_ref.shape[0] // height):
        here = pl.ds(k * height, height)
        blocks.append(pltpu.make_async_copy(stepped_ref.at[here], out_hbm.at[here], block_sem.at[k]))

        @pl.when(fragment != k)
        def _(k=k):
            blocks[k].start()

    replicas = GRID[0] * GRID[1] * GRID[2]
    outer_grad = old_global[...] - total[...] / replicas
    moved = outer_beta * old_momentum[...] + outer_grad
    new_momentum[...] = moved
    new_global[...] = old_global[...] - outer_rate * (outer_grad + outer_beta * moved)
    first = pl.ds(pl.multiple_of(fragment * height, height), height)
    last = [
        pltpu.make_async_copy(new_global, global_hbm, last_sem.at[0]),
        pltpu.make_async_copy(new_momentum, momentum_hbm, last_sem.at[1]),
        pltpu.make_async_copy(merged, out_hbm.at[first], last_sem.at[2]),
    ]
    for copy in last[:2]:
        copy.start()
    grad = lax.dot_general(
        x_ref[:, :, :, first].reshape(tokens, height), dproj[...].reshape(tokens, width),
        (((0,), (0,)), ((), ())), preferred_element_type=f32,
    )
    chosen = w_ref[first, :].astype(f32) - inner_rate * grad
    mixed = (1.0 - merge_weight) * chosen + merge_weight * new_global[...]
    merged[...] = mixed.astype(bf16)
    last[2].start()
    for k, copy in enumerate(blocks):

        @pl.when(fragment != k)
        def _(copy=copy):
            copy.wait()

    for copy in last:
        copy.wait()


def local(inputs, weights, cotangent, gain, snapshot, global_rows, momentum, plan, delay):
    tokens, features = inputs.shape
    width = weights.shape[1]
    height = snapshot.shape[0]
    chunks = CHUNKS
    step = tokens // chunks
    nz, ny, nx = GRID
    size = height // (nx * ny)
    most = max(nx, ny)
    hbm = pl.BlockSpec(memory_space=pltpu.HBM)
    vmem = pl.BlockSpec(memory_space=pltpu.VMEM)
    dma = pltpu.SemaphoreType.DMA

    def stay(value):
        return pltpu.with_memory_space_constraint(value, pltpu.HBM)

    kept = pl.pallas_call(
        exchange_kernel,
        name="exchange",
        out_shape=(
            pltpu.VMEM((4, chunks, step, features), bf16),
            pltpu.VMEM((features, width), bf16),
            pltpu.VMEM((4, chunks, step, width), bf16),
            pltpu.VMEM((features, width), bf16),
            pltpu.VMEM((height, width), f32),
            pltpu.VMEM((height, width), f32),
            pltpu.VMEM((height, width), f32),
        ),
        in_specs=[hbm] * 7,
        out_specs=(vmem,) * 7,
        scratch_shapes=[
            pltpu.VMEM((4, chunks, step, width), bf16),
            pltpu.VMEM((width,), f32),
            pltpu.VMEM((chunks, 4 * step, width), f32),
            pltpu.VMEM((features, width), f32),
            pltpu.VMEM((chunks, 8, 4 * step), f32),
            pltpu.VMEM((chunks, 3, 8, 4 * step), f32),
            pltpu.VMEM((nx * ny, size, width), bf16),
            pltpu.VMEM((nz, size, width), f32),
            dma((7,)),
            dma((chunks,)),
            dma((chunks,)),
            dma((chunks,)),
            dma((chunks,)),
            dma((chunks,)),
            dma((chunks,)),
            dma((chunks, 3)),
            dma((chunks, 3)),
            dma((nx * ny - 1,)),
            dma((nx * ny - 1,)),
            dma((nz - 1,)),
            dma((nz - 1,)),
            dma((2, most - 1)),
            dma((2, most - 1)),
            dma((2, most - 1, most - 1)),
            dma((2, most - 1, most - 1)),
        ],
        compiler_params=pltpu.CompilerParams(
            collective_id=0, has_side_effects=True, vmem_limit_bytes=32 * 2**20
        ),
    )(
        stay(inputs.reshape(chunks, step, features)),
        stay(weights),
        stay(cotangent.reshape(4, chunks, step, width)),
        stay(gain),
        stay(snapshot.reshape(nx * ny, size, width)),
        stay(global_rows),
        stay(momentum),
    )
    kept = [pltpu.with_memory_space_constraint(value, pltpu.VMEM) for value in kept]
    return pl.pallas_call(
        update_kernel,
        name="update",
        out_shape=(
            jax.ShapeDtypeStruct((features, width), bf16),
            jax.ShapeDtypeStruct((height, width), f32),
            jax.ShapeDtypeStruct((height, width), f32),
        ),
        in_specs=[vmem] * 9,
        out_specs=(hbm,) * 3,
        scratch_shapes=[
            pltpu.VMEM((height, width), f32),
            pltpu.VMEM((height, width), f32),
            pltpu.VMEM((height, width), bf16),
            dma((features // height,)),
            dma((3,)),
        ],
        compiler_params=pltpu.CompilerParams(vmem_limit_bytes=16 * 2**20),
    )(plan, delay, *kept)


def solution(mesh):
    in_specs = (
        P(("replica", "fsdp"), None),
        P("replica", "fsdp"),
        P("replica", "fsdp"),
        P("fsdp"),
        P("replica", "fsdp"),
        P(None, "fsdp"),
        P(None, "fsdp"),
        P(),
        P(),
    )
    out_specs = (P("replica", "fsdp"), P(None, "fsdp"), P(None, "fsdp"))
    return jax.shard_map(local, mesh=mesh, in_specs=in_specs, out_specs=out_specs, check_vma=False)
```

```python
import functools

import jax
import jax.numpy as jnp
from jax import lax
from jax.experimental import pallas as pl
from jax.experimental.pallas import tpu as pltpu
from jax.sharding import PartitionSpec as P

norm_eps = 1e-06
inner_rate = 0.02
outer_rate = 0.7
outer_beta = 0.9
merge_weight = 0.5

GRID = (4, 4, 4)
CHUNKS = 4
AHEAD = 2

f32 = jnp.float32
bf16 = jnp.bfloat16


def exchange_kernel(
    x_hbm, w_hbm, cot_hbm, gain_hbm, snap_hbm, global_hbm, momentum_hbm,
    x_ref, dproj, base, total, old_global, old_momentum,
    w_ref, cot, gain, proj, message, sums,
    snaps, plane,
    local_sem, sib_send, sib_recv, far_send, far_recv, fwd_send, fwd_recv,
    sum_send, sum_recv, scatter_send, scatter_recv, plane_send, plane_recv,
    gather_send, gather_recv,
):
    nz, ny, nx = GRID
    r = lax.axis_index("replica")
    f = lax.axis_index("fsdp")
    z = lax.div(r, nx * ny)
    place = lax.rem(r, nx * ny)
    core = lax.rem(f, 2)
    sibling = f + 1 - 2 * core
    far = lax.rem(f + 2, 4)
    far_sibling = 3 - f
    _, chunks, step, features = x_ref.shape
    rows = 4 * step
    width = w_ref.shape[1]
    model = 4 * width
    height = total.shape[0]
    size = height // (nx * ny)

    def plane_peer(d):
        return {"replica": r - place + lax.rem(place + d, nx * ny)}

    def z_peer(d):
        return {"replica": r + nx * ny * (lax.rem(z + d, nz) - z)}

    def fsdp_peer(which):
        return {"fsdp": which}

    sent = []

    def send(src, dst, send_sem, recv_sem, where):
        copy = pltpu.make_async_remote_copy(
            src_ref=src, dst_ref=dst, send_sem=send_sem, recv_sem=recv_sem,
            device_id=where, device_id_type=pl.DeviceIdType.MESH,
        )
        copy.start()
        sent.append(copy)
        return copy

    barrier = pltpu.get_barrier_semaphore()
    partners = [fsdp_peer(sibling), fsdp_peer(far), fsdp_peer(far_sibling)]
    partners += [plane_peer(d) for d in range(1, nx * ny)]
    partners += [z_peer(d) for d in range(1, nz)]
    for where in partners:
        pl.semaphore_signal(barrier, inc=1, device_id=where, device_id_type=pl.DeviceIdType.MESH)

    mine = []
    for which, (src, dst) in enumerate((
        (w_hbm, w_ref), (x_hbm, x_ref.at[f]), (cot_hbm, cot), (gain_hbm, gain),
        (global_hbm, old_global), (momentum_hbm, old_momentum),
    )):
        mine.append(pltpu.make_async_copy(src, dst, local_sem.at[which]))
    mine.append(pltpu.make_async_copy(snap_hbm.at[place], snaps.at[0], local_sem.at[len(mine)]))
    mine[0].start()
    pl.semaphore_wait(barrier, len(partners))

    def scatter():
        return [
            send(
                snap_hbm.at[lax.rem(place + d, nx * ny)], snaps.at[d],
                scatter_send.at[d - 1], scatter_recv.at[d - 1], plane_peer(d),
            )
            for d in range(1, nx * ny)
        ]

    def across_planes(before):
        mine[4].wait()
        mine[-1].wait()
        for copy in before:
            copy.wait_recv()
        here = old_global[pl.ds(pl.multiple_of(place * size, size), size), :]
        amount = here - snaps[0].astype(f32)
        for k in range(1, nx * ny):
            amount += here - snaps[k].astype(f32)
        plane[z] = amount.astype(bf16)
        return [
            send(plane.at[z], plane.at[z], plane_send.at[d - 1], plane_recv.at[d - 1], z_peer(d))
            for d in range(1, nz)
        ]

    def gather(before):
        for copy in before:
            copy.wait_recv()
        amount = plane[0].astype(f32)
        for k in range(1, nz):
            amount += plane[k].astype(f32)
        here = total.at[pl.ds(pl.multiple_of(place * size, size), size)]
        here[...] = amount
        return [
            send(here, here, gather_send.at[d - 1], gather_recv.at[d - 1], plane_peer(d))
            for d in range(1, nx * ny)
        ]

    def scaled_of(c):
        return cot[:, c].reshape(rows, width).astype(f32) * (1.0 + gain[...].reshape(1, width))

    def lanes(value):
        amount = value[:, :128]
        for k in range(128, width, 128):
            amount += value[:, k : k + 128]
        return jnp.sum(amount.T, axis=0, keepdims=True)

    def project(c):
        tokens = x_ref[:, c].reshape(rows, features)
        value = jnp.dot(tokens, w_ref[...], preferred_element_type=f32)
        proj[c] = value
        message[c, 0:1, :] = lanes(value * value)
        message[c, 1:2, :] = lanes(scaled_of(c) * value)
        return [
            send(
                message.at[c], sums.at[c, d], sum_send.at[c, d], sum_recv.at[c, d], fsdp_peer(where)
            )
            for d, where in enumerate((sibling, far, far_sibling))
        ]

    def column(value):
        return jnp.broadcast_to(value, (128, rows)).T

    def finish(c, before):
        for copy in before:
            copy.wait_recv()
        both = message[c] + sums[c, 0] + sums[c, 1] + sums[c, 2]
        inverse = lax.rsqrt(both[0:1] / model + norm_eps)
        factor = inverse * inverse * inverse * (both[1:2] / model)
        inverse, factor = column(inverse), column(factor)
        scaled = scaled_of(c)
        for k in range(0, width, 128):
            value = inverse * scaled[:, k : k + 128] - proj[c, :, k : k + 128] * factor
            dproj[:, c, :, k : k + 128] = value.astype(bf16).reshape(4, step, 128)

    def begin_update():
        half = chunks // 2
        right = dproj[:, :half].reshape(half * rows, width)
        tile = min(256, features)
        for k in range(0, features, tile):
            left = x_ref[:, :half, :, k : k + tile].reshape(half * rows, tile)
            value = lax.dot_general(
                left, right, (((0,), (0,)), ((), ())), preferred_element_type=f32
            )
            base[k : k + tile] = w_ref[k : k + tile].astype(f32) - inner_rate * value

    def x_part(c, sems, where):
        return send(x_hbm.at[c], x_ref.at[f, c], sems[0].at[c], sems[1].at[c], fsdp_peer(where))

    scattered = scatter()
    far_copy = [x_part(c, (far_send, far_recv), far) for c in range(min(AHEAD, chunks))]
    for copy in mine[1:]:
        copy.start()
    sib_copy = [x_part(c, (sib_send, sib_recv), sibling) for c in range(chunks)]
    message[...] = jnp.zeros_like(message)

    def forward(c):
        far_copy[c].wait_recv()
        if len(far_copy) < chunks:
            far_copy.append(x_part(len(far_copy), (far_send, far_recv), far))
        part = x_ref.at[far, c]
        return send(part, part, fwd_send.at[c], fwd_recv.at[c], fsdp_peer(sibling))

    def wave(c, copy):
        sib_copy[c].wait_recv()
        copy.wait_recv()
        return project(c)

    copy = forward(0)
    planes = across_planes(scattered)
    for local_copy in mine[:4]:
        local_copy.wait()
    last = chunks - 1
    summing = [wave(0, copy)]
    copy = forward(1)
    summing.append(wave(1, copy))
    finish(0, summing[0])
    copy = forward(2)
    pieces = gather(planes)
    summing.append(wave(2, copy))
    finish(1, summing[1])
    copy = forward(last)
    summing.append(wave(last, copy))
    begin_update()
    finish(last - 1, summing[last - 1])
    finish(last, summing[last])
    for local_copy in mine[5:-1]:
        local_copy.wait()
    for copy in pieces:
        copy.wait_recv()
    for copy in sent:
        copy.wait_send()


def update_kernel(
    plan_ref, delay_ref, x_ref, dproj, base, total, old_global, old_momentum,
    out_hbm, global_hbm, momentum_hbm, stepped, new_global, new_momentum, merged, block_sem, last_sem,
):
    height, width = total.shape
    features = base.shape[0]
    _, chunks, step, _ = x_ref.shape
    half = chunks // 2
    rows = 4 * (chunks - half) * step
    plan = plan_ref[...].reshape(1, plan_ref.shape[0])
    position = plan.shape[1] - 1 - delay_ref[...].reshape(1, 1)
    chosen = lax.broadcasted_iota(jnp.int32, plan.shape, 1) == position
    fragment = jnp.sum(jnp.where(chosen, plan, 0))
    right = dproj[:, half:].reshape(rows, width)

    def finished(here, count):
        left = x_ref[:, half:, :, here].reshape(rows, count)
        grad = lax.dot_general(left, right, (((0,), (0,)), ((), ())), preferred_element_type=f32)
        return base[here, :] - inner_rate * grad

    tile = min(256, features)
    blocks = []
    for i in range(0, features, tile):
        stepped[i : i + tile] = finished(pl.ds(i, tile), tile).astype(bf16)
        for k in range(i // height, (i + tile) // height):
            here = pl.ds(k * height, height)
            blocks.append(pltpu.make_async_copy(stepped.at[here], out_hbm.at[here], block_sem.at[k]))

            @pl.when(fragment != k)
            def _(k=k):
                blocks[k].start()

    replicas = GRID[0] * GRID[1] * GRID[2]
    outer_grad = total[...] / replicas
    moved = outer_beta * old_momentum[...] + outer_grad
    new_momentum[...] = moved
    new_global[...] = old_global[...] - outer_rate * (outer_grad + outer_beta * moved)
    first = pl.ds(pl.multiple_of(fragment * height, height), height)
    last = [
        pltpu.make_async_copy(new_global, global_hbm, last_sem.at[0]),
        pltpu.make_async_copy(new_momentum, momentum_hbm, last_sem.at[1]),
        pltpu.make_async_copy(merged, out_hbm.at[first], last_sem.at[2]),
    ]
    for copy in last[:2]:
        copy.start()
    mixed = (1.0 - merge_weight) * finished(first, height) + merge_weight * new_global[...]
    merged[...] = mixed.astype(bf16)
    last[2].start()
    for k, copy in enumerate(blocks):

        @pl.when(fragment != k)
        def _(copy=copy):
            copy.wait()

    for copy in last:
        copy.wait()


def local(inputs, weights, cotangent, gain, snapshot, global_rows, momentum, plan, delay):
    tokens, features = inputs.shape
    width = weights.shape[1]
    height = snapshot.shape[0]
    chunks = CHUNKS
    step = tokens // chunks
    nz, ny, nx = GRID
    size = height // (nx * ny)
    hbm = pl.BlockSpec(memory_space=pltpu.HBM)
    vmem = pl.BlockSpec(memory_space=pltpu.VMEM)
    dma = pltpu.SemaphoreType.DMA

    def stay(value):
        return pltpu.with_memory_space_constraint(value, pltpu.HBM)

    kept = pl.pallas_call(
        exchange_kernel,
        name="exchange",
        out_shape=(
            pltpu.VMEM((4, chunks, step, features), bf16),
            pltpu.VMEM((4, chunks, step, width), bf16),
            pltpu.VMEM((features, width), f32),
            pltpu.VMEM((height, width), f32),
            pltpu.VMEM((height, width), f32),
            pltpu.VMEM((height, width), f32),
        ),
        in_specs=[hbm] * 7,
        out_specs=(vmem,) * 6,
        scratch_shapes=[
            pltpu.VMEM((features, width), bf16),
            pltpu.VMEM((4, chunks, step, width), bf16),
            pltpu.VMEM((width,), f32),
            pltpu.VMEM((chunks, 4 * step, width), f32),
            pltpu.VMEM((chunks, 8, 4 * step), f32),
            pltpu.VMEM((chunks, 3, 8, 4 * step), f32),
            pltpu.VMEM((nx * ny, size, width), bf16),
            pltpu.VMEM((nz, size, width), bf16),
            dma((7,)),
            dma((chunks,)),
            dma((chunks,)),
            dma((chunks,)),
            dma((chunks,)),
            dma((chunks,)),
            dma((chunks,)),
            dma((chunks, 3)),
            dma((chunks, 3)),
            dma((nx * ny - 1,)),
            dma((nx * ny - 1,)),
            dma((nz - 1,)),
            dma((nz - 1,)),
            dma((nx * ny - 1,)),
            dma((nx * ny - 1,)),
        ],
        compiler_params=pltpu.CompilerParams(
            collective_id=0, has_side_effects=True, vmem_limit_bytes=32 * 2**20
        ),
    )(
        stay(inputs.reshape(chunks, step, features)),
        stay(weights),
        stay(cotangent.reshape(4, chunks, step, width)),
        stay(gain),
        stay(snapshot.reshape(nx * ny, size, width)),
        stay(global_rows),
        stay(momentum),
    )
    kept = [pltpu.with_memory_space_constraint(value, pltpu.VMEM) for value in kept]
    return pl.pallas_call(
        update_kernel,
        name="update",
        out_shape=(
            jax.ShapeDtypeStruct((features, width), bf16),
            jax.ShapeDtypeStruct((height, width), f32),
            jax.ShapeDtypeStruct((height, width), f32),
        ),
        in_specs=[vmem] * 8,
        out_specs=(hbm,) * 3,
        scratch_shapes=[
            pltpu.VMEM((features, width), bf16),
            pltpu.VMEM((height, width), f32),
            pltpu.VMEM((height, width), f32),
            pltpu.VMEM((height, width), bf16),
            dma((features // height,)),
            dma((3,)),
        ],
        compiler_params=pltpu.CompilerParams(vmem_limit_bytes=16 * 2**20),
    )(plan, delay, *kept)


def solution(mesh):
    in_specs = (
        P(("replica", "fsdp"), None),
        P("replica", "fsdp"),
        P("replica", "fsdp"),
        P("fsdp"),
        P("replica", "fsdp"),
        P(None, "fsdp"),
        P(None, "fsdp"),
        P(),
        P(),
    )
    out_specs = (P("replica", "fsdp"), P(None, "fsdp"), P(None, "fsdp"))
    return jax.shard_map(local, mesh=mesh, in_specs=in_specs, out_specs=out_specs, check_vma=False)
```

```python
import functools

import jax
import jax.numpy as jnp
from jax import lax
from jax.experimental import pallas as pl
from jax.experimental.pallas import tpu as pltpu
from jax.sharding import PartitionSpec as P

norm_eps = 1e-06
inner_rate = 0.02
outer_rate = 0.7
outer_beta = 0.9
merge_weight = 0.5

GRID = (4, 4, 4)
CHUNKS = 4
AHEAD = 3
PARTS = 2

f32 = jnp.float32
bf16 = jnp.bfloat16


def exchange_kernel(
    x_hbm, w_hbm, cot_hbm, gain_hbm, snap_hbm, global_hbm, momentum_hbm,
    x_ref, dproj, base, total, old_global, old_momentum,
    w_ref, cot, gain, proj, message, sums,
    snaps, plane,
    local_sem, sib_send, sib_recv, far_send, far_recv, fwd_send, fwd_recv,
    sum_send, sum_recv, scatter_send, scatter_recv, plane_send, plane_recv,
    gather_send, gather_recv,
):
    nz, ny, nx = GRID
    r = lax.axis_index("replica")
    f = lax.axis_index("fsdp")
    z = lax.div(r, nx * ny)
    place = lax.rem(r, nx * ny)
    core = lax.rem(f, 2)
    sibling = f + 1 - 2 * core
    far = lax.rem(f + 2, 4)
    far_sibling = 3 - f
    _, chunks, step, features = x_ref.shape
    rows = 4 * step
    width = w_ref.shape[1]
    model = 4 * width
    height = total.shape[0]
    size = height // (nx * ny)

    def plane_peer(d):
        return {"replica": r - place + lax.rem(place + d, nx * ny)}

    def z_peer(d):
        return {"replica": r + nx * ny * (lax.rem(z + d, nz) - z)}

    def fsdp_peer(which):
        return {"fsdp": which}

    sent = []

    def send(src, dst, send_sem, recv_sem, where):
        copy = pltpu.make_async_remote_copy(
            src_ref=src, dst_ref=dst, send_sem=send_sem, recv_sem=recv_sem,
            device_id=where, device_id_type=pl.DeviceIdType.MESH,
        )
        copy.start()
        sent.append(copy)
        return copy

    barrier = pltpu.get_barrier_semaphore()
    partners = [fsdp_peer(sibling), fsdp_peer(far), fsdp_peer(far_sibling)]
    partners += [plane_peer(d) for d in range(1, nx * ny)]
    partners += [z_peer(d) for d in range(1, nz)]
    for where in partners:
        pl.semaphore_signal(barrier, inc=1, device_id=where, device_id_type=pl.DeviceIdType.MESH)

    mine = []
    for which, (src, dst) in enumerate((
        (w_hbm, w_ref), (x_hbm, x_ref.at[f]), (cot_hbm, cot), (gain_hbm, gain),
        (global_hbm, old_global), (momentum_hbm, old_momentum),
    )):
        mine.append(pltpu.make_async_copy(src, dst, local_sem.at[which]))
    mine.append(pltpu.make_async_copy(snap_hbm.at[place], snaps.at[0], local_sem.at[len(mine)]))
    mine[0].start()
    pl.semaphore_wait(barrier, len(partners))

    def scatter():
        return [
            send(
                snap_hbm.at[lax.rem(place + d, nx * ny)], snaps.at[d],
                scatter_send.at[d - 1], scatter_recv.at[d - 1], plane_peer(d),
            )
            for d in range(1, nx * ny)
        ]

    def across_planes(before):
        mine[4].wait()
        mine[-1].wait()
        for copy in before:
            copy.wait_recv()
        here = old_global[pl.ds(pl.multiple_of(place * size, size), size), :]
        amount = here - snaps[0].astype(f32)
        for k in range(1, nx * ny):
            amount += here - snaps[k].astype(f32)
        plane[z] = amount.astype(bf16)
        return [
            send(plane.at[z], plane.at[z], plane_send.at[d - 1], plane_recv.at[d - 1], z_peer(d))
            for d in range(1, nz)
        ]

    def gather(before):
        for copy in before:
            copy.wait_recv()
        amount = plane[0].astype(f32)
        for k in range(1, nz):
            amount += plane[k].astype(f32)
        here = total.at[pl.ds(pl.multiple_of(place * size, size), size)]
        here[...] = amount
        return [
            send(here, here, gather_send.at[d - 1], gather_recv.at[d - 1], plane_peer(d))
            for d in range(1, nx * ny)
        ]

    def scaled_of(c):
        return cot[:, c].reshape(rows, width).astype(f32) * (1.0 + gain[...].reshape(1, width))

    def lanes(value):
        amount = value[:, :128]
        for k in range(128, width, 128):
            amount += value[:, k : k + 128]
        return jnp.sum(amount.T, axis=0, keepdims=True)

    def project(c):
        tokens = x_ref[:, c].reshape(rows, features)
        value = jnp.dot(tokens, w_ref[...], preferred_element_type=f32)
        proj[c] = value
        message[c, 0:1, :] = lanes(value * value)
        message[c, 1:2, :] = lanes(scaled_of(c) * value)
        return [
            send(
                message.at[c], sums.at[c, d], sum_send.at[c, d], sum_recv.at[c, d], fsdp_peer(where)
            )
            for d, where in enumerate((sibling, far, far_sibling))
        ]

    def column(value):
        return jnp.broadcast_to(value, (128, rows)).T

    def finish(c, before):
        for copy in before:
            copy.wait_recv()
        both = message[c] + sums[c, 0] + sums[c, 1] + sums[c, 2]
        inverse = lax.rsqrt(both[0:1] / model + norm_eps)
        factor = inverse * inverse * inverse * (both[1:2] / model)
        inverse, factor = column(inverse), column(factor)
        scaled = scaled_of(c)
        for k in range(0, width, 128):
            value = inverse * scaled[:, k : k + 128] - proj[c, :, k : k + 128] * factor
            dproj[:, c, :, k : k + 128] = value.astype(bf16).reshape(4, step, 128)

    def begin_update():
        half = chunks // 2
        right = dproj[:, :half].reshape(half * rows, width)
        tile = min(256, features)
        for k in range(0, features, tile):
            left = x_ref[:, :half, :, k : k + tile].reshape(half * rows, tile)
            value = lax.dot_general(
                left, right, (((0,), (0,)), ((), ())), preferred_element_type=f32
            )
            base[k : k + tile] = w_ref[k : k + tile].astype(f32) - inner_rate * value

    piece = step // PARTS
    parts = chunks * PARTS

    def lines(p):
        return p // PARTS, pl.ds(p % PARTS * piece, piece)

    def x_part(p):
        c, here = lines(p)
        return send(
            x_hbm.at[c, here], x_ref.at[f, c, here], far_send.at[p], far_recv.at[p], fsdp_peer(far)
        )

    def x_chunk(c):
        return send(x_hbm.at[c], x_ref.at[f, c], sib_send.at[c], sib_recv.at[c], fsdp_peer(sibling))

    scattered = scatter()
    far_copy = [x_part(p) for p in range(min(AHEAD, parts))]
    for copy in mine[1:]:
        copy.start()
    sib_copy = [x_chunk(c) for c in range(chunks)]
    message[...] = jnp.zeros_like(message)

    def pass_on(p):
        far_copy[p].wait_recv()
        if len(far_copy) < parts:
            far_copy.append(x_part(len(far_copy)))
        c, here = lines(p)
        part = x_ref.at[far, c, here]
        return send(part, part, fwd_send.at[p], fwd_recv.at[p], fsdp_peer(sibling))

    def forward(c):
        return [pass_on(p) for p in range(c * PARTS, (c + 1) * PARTS)]

    def wave(c, copies):
        sib_copy[c].wait_recv()
        for copy in copies:
            copy.wait_recv()
        return project(c)

    copy = forward(0)
    planes = across_planes(scattered)
    for local_copy in mine[:4]:
        local_copy.wait()
    last = chunks - 1
    summing = [wave(0, copy)]
    copy = forward(1)
    summing.append(wave(1, copy))
    finish(0, summing[0])
    copy = forward(2)
    pieces = gather(planes)
    summing.append(wave(2, copy))
    finish(1, summing[1])
    copy = forward(last)
    summing.append(wave(last, copy))
    begin_update()
    finish(last - 1, summing[last - 1])
    finish(last, summing[last])
    for local_copy in mine[5:-1]:
        local_copy.wait()
    for copy in pieces:
        copy.wait_recv()
    for copy in sent:
        copy.wait_send()


def update_kernel(
    plan_ref, delay_ref, x_ref, dproj, base, total, old_global, old_momentum,
    out_hbm, global_hbm, momentum_hbm, stepped, new_global, new_momentum, merged, block_sem, last_sem,
):
    height, width = total.shape
    features = base.shape[0]
    _, chunks, step, _ = x_ref.shape
    half = chunks // 2
    rows = 4 * (chunks - half) * step
    plan = plan_ref[...].reshape(1, plan_ref.shape[0])
    position = plan.shape[1] - 1 - delay_ref[...].reshape(1, 1)
    chosen = lax.broadcasted_iota(jnp.int32, plan.shape, 1) == position
    fragment = jnp.sum(jnp.where(chosen, plan, 0))
    right = dproj[:, half:].reshape(rows, width)

    def finished(here, count):
        left = x_ref[:, half:, :, here].reshape(rows, count)
        grad = lax.dot_general(left, right, (((0,), (0,)), ((), ())), preferred_element_type=f32)
        return base[here, :] - inner_rate * grad

    tile = min(256, features)
    blocks = []
    for i in range(0, features, tile):
        stepped[i : i + tile] = finished(pl.ds(i, tile), tile).astype(bf16)
        for k in range(i // height, (i + tile) // height):
            here = pl.ds(k * height, height)
            blocks.append(pltpu.make_async_copy(stepped.at[here], out_hbm.at[here], block_sem.at[k]))

            @pl.when(fragment != k)
            def _(k=k):
                blocks[k].start()

    replicas = GRID[0] * GRID[1] * GRID[2]
    outer_grad = total[...] / replicas
    moved = outer_beta * old_momentum[...] + outer_grad
    new_momentum[...] = moved
    new_global[...] = old_global[...] - outer_rate * (outer_grad + outer_beta * moved)
    first = pl.ds(pl.multiple_of(fragment * height, height), height)
    last = [
        pltpu.make_async_copy(new_global, global_hbm, last_sem.at[0]),
        pltpu.make_async_copy(new_momentum, momentum_hbm, last_sem.at[1]),
        pltpu.make_async_copy(merged, out_hbm.at[first], last_sem.at[2]),
    ]
    for copy in last[:2]:
        copy.start()
    mixed = (1.0 - merge_weight) * finished(first, height) + merge_weight * new_global[...]
    merged[...] = mixed.astype(bf16)
    last[2].start()
    for k, copy in enumerate(blocks):

        @pl.when(fragment != k)
        def _(copy=copy):
            copy.wait()

    for copy in last:
        copy.wait()


def local(inputs, weights, cotangent, gain, snapshot, global_rows, momentum, plan, delay):
    tokens, features = inputs.shape
    width = weights.shape[1]
    height = snapshot.shape[0]
    chunks = CHUNKS
    step = tokens // chunks
    nz, ny, nx = GRID
    size = height // (nx * ny)
    hbm = pl.BlockSpec(memory_space=pltpu.HBM)
    vmem = pl.BlockSpec(memory_space=pltpu.VMEM)
    dma = pltpu.SemaphoreType.DMA

    def stay(value):
        return pltpu.with_memory_space_constraint(value, pltpu.HBM)

    kept = pl.pallas_call(
        exchange_kernel,
        name="exchange",
        out_shape=(
            pltpu.VMEM((4, chunks, step, features), bf16),
            pltpu.VMEM((4, chunks, step, width), bf16),
            pltpu.VMEM((features, width), f32),
            pltpu.VMEM((height, width), f32),
            pltpu.VMEM((height, width), f32),
            pltpu.VMEM((height, width), f32),
        ),
        in_specs=[hbm] * 7,
        out_specs=(vmem,) * 6,
        scratch_shapes=[
            pltpu.VMEM((features, width), bf16),
            pltpu.VMEM((4, chunks, step, width), bf16),
            pltpu.VMEM((width,), f32),
            pltpu.VMEM((chunks, 4 * step, width), f32),
            pltpu.VMEM((chunks, 8, 4 * step), f32),
            pltpu.VMEM((chunks, 3, 8, 4 * step), f32),
            pltpu.VMEM((nx * ny, size, width), bf16),
            pltpu.VMEM((nz, size, width), bf16),
            dma((7,)),
            dma((chunks,)),
            dma((chunks,)),
            dma((chunks * PARTS,)),
            dma((chunks * PARTS,)),
            dma((chunks * PARTS,)),
            dma((chunks * PARTS,)),
            dma((chunks, 3)),
            dma((chunks, 3)),
            dma((nx * ny - 1,)),
            dma((nx * ny - 1,)),
            dma((nz - 1,)),
            dma((nz - 1,)),
            dma((nx * ny - 1,)),
            dma((nx * ny - 1,)),
        ],
        compiler_params=pltpu.CompilerParams(
            collective_id=0, has_side_effects=True, vmem_limit_bytes=32 * 2**20
        ),
    )(
        stay(inputs.reshape(chunks, step, features)),
        stay(weights),
        stay(cotangent.reshape(4, chunks, step, width)),
        stay(gain),
        stay(snapshot.reshape(nx * ny, size, width)),
        stay(global_rows),
        stay(momentum),
    )
    kept = [pltpu.with_memory_space_constraint(value, pltpu.VMEM) for value in kept]
    return pl.pallas_call(
        update_kernel,
        name="update",
        out_shape=(
            jax.ShapeDtypeStruct((features, width), bf16),
            jax.ShapeDtypeStruct((height, width), f32),
            jax.ShapeDtypeStruct((height, width), f32),
        ),
        in_specs=[vmem] * 8,
        out_specs=(hbm,) * 3,
        scratch_shapes=[
            pltpu.VMEM((features, width), bf16),
            pltpu.VMEM((height, width), f32),
            pltpu.VMEM((height, width), f32),
            pltpu.VMEM((height, width), bf16),
            dma((features // height,)),
            dma((3,)),
        ],
        compiler_params=pltpu.CompilerParams(vmem_limit_bytes=16 * 2**20),
    )(plan, delay, *kept)


def solution(mesh):
    in_specs = (
        P(("replica", "fsdp"), None),
        P("replica", "fsdp"),
        P("replica", "fsdp"),
        P("fsdp"),
        P("replica", "fsdp"),
        P(None, "fsdp"),
        P(None, "fsdp"),
        P(),
        P(),
    )
    out_specs = (P("replica", "fsdp"), P(None, "fsdp"), P(None, "fsdp"))
    return jax.shard_map(local, mesh=mesh, in_specs=in_specs, out_specs=out_specs, check_vma=False)
```

```python
import functools

import jax
import jax.numpy as jnp
from jax import lax
from jax.experimental import pallas as pl
from jax.experimental.pallas import tpu as pltpu
from jax.sharding import PartitionSpec as P

norm_eps = 1e-06
inner_rate = 0.02
outer_rate = 0.7
outer_beta = 0.9
merge_weight = 0.5

GRID = (4, 4, 4)
CHUNKS = 4
AHEAD = 3
PARTS = 2

f32 = jnp.float32
bf16 = jnp.bfloat16


def exchange_kernel(
    x_hbm, w_hbm, cot_hbm, gain_hbm, snap_hbm, global_hbm, momentum_hbm,
    x_ref, dproj, base, total, old_global, old_momentum,
    w_ref, cot, gain, proj, message, sums,
    snaps, plane,
    local_sem, sib_send, sib_recv, far_send, far_recv, fwd_send, fwd_recv,
    sum_send, sum_recv, scatter_send, scatter_recv, plane_send, plane_recv,
    gather_send, gather_recv,
):
    nz, ny, nx = GRID
    r = lax.axis_index("replica")
    f = lax.axis_index("fsdp")
    z = lax.div(r, nx * ny)
    place = lax.rem(r, nx * ny)
    core = lax.rem(f, 2)
    sibling = f + 1 - 2 * core
    far = lax.rem(f + 2, 4)
    far_sibling = 3 - f
    _, chunks, step, features = x_ref.shape
    rows = 4 * step
    width = w_ref.shape[1]
    model = 4 * width
    height = total.shape[0]
    size = height // (nx * ny)

    x, y = lax.rem(place, nx), lax.div(place, nx)
    hops = [min(d % nx, nx - d % nx) + min(d // nx, ny - d // nx) for d in range(nx * ny)]
    farthest_first = sorted(range(1, nx * ny), key=lambda d: -hops[d])

    def plane_place(d):
        return lax.rem(x + d % nx, nx) + nx * lax.rem(y + d // nx, ny)

    def plane_peer(d):
        return {"replica": r - place + plane_place(d)}

    def z_peer(d):
        return {"replica": r + nx * ny * (lax.rem(z + d, nz) - z)}

    def fsdp_peer(which):
        return {"fsdp": which}

    sent = []

    def send(src, dst, send_sem, recv_sem, where):
        copy = pltpu.make_async_remote_copy(
            src_ref=src, dst_ref=dst, send_sem=send_sem, recv_sem=recv_sem,
            device_id=where, device_id_type=pl.DeviceIdType.MESH,
        )
        copy.start()
        sent.append(copy)
        return copy

    barrier = pltpu.get_barrier_semaphore()
    partners = [fsdp_peer(sibling), fsdp_peer(far), fsdp_peer(far_sibling)]
    partners += [plane_peer(d) for d in range(1, nx * ny)]
    partners += [z_peer(d) for d in range(1, nz)]
    for where in partners:
        pl.semaphore_signal(barrier, inc=1, device_id=where, device_id_type=pl.DeviceIdType.MESH)

    mine = []
    for which, (src, dst) in enumerate((
        (w_hbm, w_ref), (x_hbm, x_ref.at[f]), (cot_hbm, cot), (gain_hbm, gain),
        (global_hbm, old_global), (momentum_hbm, old_momentum),
    )):
        mine.append(pltpu.make_async_copy(src, dst, local_sem.at[which]))
    mine.append(pltpu.make_async_copy(snap_hbm.at[place], snaps.at[0], local_sem.at[len(mine)]))
    mine[0].start()
    pl.semaphore_wait(barrier, len(partners))

    def scatter():
        return [
            send(
                snap_hbm.at[plane_place(d)], snaps.at[d],
                scatter_send.at[d - 1], scatter_recv.at[d - 1], plane_peer(d),
            )
            for d in farthest_first
        ]

    def across_planes(before):
        mine[4].wait()
        mine[-1].wait()
        for copy in before:
            copy.wait_recv()
        here = old_global[pl.ds(pl.multiple_of(place * size, size), size), :]
        amount = here - snaps[0].astype(f32)
        for k in range(1, nx * ny):
            amount += here - snaps[k].astype(f32)
        plane[z] = amount.astype(bf16)
        return [
            send(plane.at[z], plane.at[z], plane_send.at[d - 1], plane_recv.at[d - 1], z_peer(d))
            for d in range(1, nz)
        ]

    def gather(before):
        for copy in before:
            copy.wait_recv()
        amount = plane[0].astype(f32)
        for k in range(1, nz):
            amount += plane[k].astype(f32)
        here = total.at[pl.ds(pl.multiple_of(place * size, size), size)]
        here[...] = amount
        return [
            send(here, here, gather_send.at[d - 1], gather_recv.at[d - 1], plane_peer(d))
            for d in farthest_first
        ]

    def scaled_of(c):
        return cot[:, c].reshape(rows, width).astype(f32) * (1.0 + gain[...].reshape(1, width))

    def lanes(value):
        amount = value[:, :128]
        for k in range(128, width, 128):
            amount += value[:, k : k + 128]
        return jnp.sum(amount.T, axis=0, keepdims=True)

    def project(c):
        tokens = x_ref[:, c].reshape(rows, features)
        value = jnp.dot(tokens, w_ref[...], preferred_element_type=f32)
        proj[c] = value
        message[c, 0:1, :] = lanes(value * value)
        message[c, 1:2, :] = lanes(scaled_of(c) * value)
        return [
            send(
                message.at[c], sums.at[c, d], sum_send.at[c, d], sum_recv.at[c, d], fsdp_peer(where)
            )
            for d, where in enumerate((sibling, far, far_sibling))
        ]

    def column(value):
        return jnp.broadcast_to(value, (128, rows)).T

    def finish(c, before):
        for copy in before:
            copy.wait_recv()
        both = message[c] + sums[c, 0] + sums[c, 1] + sums[c, 2]
        inverse = lax.rsqrt(both[0:1] / model + norm_eps)
        factor = inverse * inverse * inverse * (both[1:2] / model)
        inverse, factor = column(inverse), column(factor)
        scaled = scaled_of(c)
        for k in range(0, width, 128):
            value = inverse * scaled[:, k : k + 128] - proj[c, :, k : k + 128] * factor
            dproj[:, c, :, k : k + 128] = value.astype(bf16).reshape(4, step, 128)

    def begin_update():
        half = chunks // 2
        right = dproj[:, :half].reshape(half * rows, width)
        tile = min(256, features)
        for k in range(0, features, tile):
            left = x_ref[:, :half, :, k : k + tile].reshape(half * rows, tile)
            value = lax.dot_general(
                left, right, (((0,), (0,)), ((), ())), preferred_element_type=f32
            )
            base[k : k + tile] = w_ref[k : k + tile].astype(f32) - inner_rate * value

    piece = step // PARTS
    parts = chunks * PARTS

    def lines(p):
        return p // PARTS, pl.ds(p % PARTS * piece, piece)

    def x_part(p):
        c, here = lines(p)
        return send(
            x_hbm.at[c, here], x_ref.at[f, c, here], far_send.at[p], far_recv.at[p], fsdp_peer(far)
        )

    def x_chunk(c):
        return send(x_hbm.at[c], x_ref.at[f, c], sib_send.at[c], sib_recv.at[c], fsdp_peer(sibling))

    scattered = scatter()
    far_copy = [x_part(p) for p in range(min(AHEAD, parts))]
    for copy in mine[1:]:
        copy.start()
    sib_copy = [x_chunk(c) for c in range(chunks)]
    message[...] = jnp.zeros_like(message)

    def pass_on(p):
        far_copy[p].wait_recv()
        if len(far_copy) < parts:
            far_copy.append(x_part(len(far_copy)))
        c, here = lines(p)
        part = x_ref.at[far, c, here]
        return send(part, part, fwd_send.at[p], fwd_recv.at[p], fsdp_peer(sibling))

    def forward(c):
        return [pass_on(p) for p in range(c * PARTS, (c + 1) * PARTS)]

    def wave(c, copies):
        sib_copy[c].wait_recv()
        for copy in copies:
            copy.wait_recv()
        return project(c)

    copy = forward(0)
    planes = across_planes(scattered)
    for local_copy in mine[:4]:
        local_copy.wait()
    last = chunks - 1
    summing = [wave(0, copy)]
    copy = forward(1)
    summing.append(wave(1, copy))
    finish(0, summing[0])
    copy = forward(2)
    pieces = gather(planes)
    summing.append(wave(2, copy))
    finish(1, summing[1])
    copy = forward(last)
    summing.append(wave(last, copy))
    begin_update()
    finish(last - 1, summing[last - 1])
    finish(last, summing[last])
    for local_copy in mine[5:-1]:
        local_copy.wait()
    for copy in pieces:
        copy.wait_recv()
    for copy in sent:
        copy.wait_send()


def update_kernel(
    plan_ref, delay_ref, x_ref, dproj, base, total, old_global, old_momentum,
    out_hbm, global_hbm, momentum_hbm, stepped, new_global, new_momentum, merged, block_sem, last_sem,
):
    height, width = total.shape
    features = base.shape[0]
    _, chunks, step, _ = x_ref.shape
    half = chunks // 2
    rows = 4 * (chunks - half) * step
    plan = plan_ref[...].reshape(1, plan_ref.shape[0])
    position = plan.shape[1] - 1 - delay_ref[...].reshape(1, 1)
    chosen = lax.broadcasted_iota(jnp.int32, plan.shape, 1) == position
    fragment = jnp.sum(jnp.where(chosen, plan, 0))
    right = dproj[:, half:].reshape(rows, width)

    def finished(here, count):
        left = x_ref[:, half:, :, here].reshape(rows, count)
        grad = lax.dot_general(left, right, (((0,), (0,)), ((), ())), preferred_element_type=f32)
        return base[here, :] - inner_rate * grad

    tile = min(256, features)
    blocks = []
    for i in range(0, features, tile):
        stepped[i : i + tile] = finished(pl.ds(i, tile), tile).astype(bf16)
        for k in range(i // height, (i + tile) // height):
            here = pl.ds(k * height, height)
            blocks.append(pltpu.make_async_copy(stepped.at[here], out_hbm.at[here], block_sem.at[k]))

            @pl.when(fragment != k)
            def _(k=k):
                blocks[k].start()

    replicas = GRID[0] * GRID[1] * GRID[2]
    outer_grad = total[...] / replicas
    moved = outer_beta * old_momentum[...] + outer_grad
    new_momentum[...] = moved
    new_global[...] = old_global[...] - outer_rate * (outer_grad + outer_beta * moved)
    first = pl.ds(pl.multiple_of(fragment * height, height), height)
    last = [
        pltpu.make_async_copy(new_global, global_hbm, last_sem.at[0]),
        pltpu.make_async_copy(new_momentum, momentum_hbm, last_sem.at[1]),
        pltpu.make_async_copy(merged, out_hbm.at[first], last_sem.at[2]),
    ]
    for copy in last[:2]:
        copy.start()
    mixed = (1.0 - merge_weight) * finished(first, height) + merge_weight * new_global[...]
    merged[...] = mixed.astype(bf16)
    last[2].start()
    for k, copy in enumerate(blocks):

        @pl.when(fragment != k)
        def _(copy=copy):
            copy.wait()

    for copy in last:
        copy.wait()


def local(inputs, weights, cotangent, gain, snapshot, global_rows, momentum, plan, delay):
    tokens, features = inputs.shape
    width = weights.shape[1]
    height = snapshot.shape[0]
    chunks = CHUNKS
    step = tokens // chunks
    nz, ny, nx = GRID
    size = height // (nx * ny)
    hbm = pl.BlockSpec(memory_space=pltpu.HBM)
    vmem = pl.BlockSpec(memory_space=pltpu.VMEM)
    dma = pltpu.SemaphoreType.DMA

    def stay(value):
        return pltpu.with_memory_space_constraint(value, pltpu.HBM)

    kept = pl.pallas_call(
        exchange_kernel,
        name="exchange",
        out_shape=(
            pltpu.VMEM((4, chunks, step, features), bf16),
            pltpu.VMEM((4, chunks, step, width), bf16),
            pltpu.VMEM((features, width), f32),
            pltpu.VMEM((height, width), f32),
            pltpu.VMEM((height, width), f32),
            pltpu.VMEM((height, width), f32),
        ),
        in_specs=[hbm] * 7,
        out_specs=(vmem,) * 6,
        scratch_shapes=[
            pltpu.VMEM((features, width), bf16),
            pltpu.VMEM((4, chunks, step, width), bf16),
            pltpu.VMEM((width,), f32),
            pltpu.VMEM((chunks, 4 * step, width), f32),
            pltpu.VMEM((chunks, 8, 4 * step), f32),
            pltpu.VMEM((chunks, 3, 8, 4 * step), f32),
            pltpu.VMEM((nx * ny, size, width), bf16),
            pltpu.VMEM((nz, size, width), bf16),
            dma((7,)),
            dma((chunks,)),
            dma((chunks,)),
            dma((chunks * PARTS,)),
            dma((chunks * PARTS,)),
            dma((chunks * PARTS,)),
            dma((chunks * PARTS,)),
            dma((chunks, 3)),
            dma((chunks, 3)),
            dma((nx * ny - 1,)),
            dma((nx * ny - 1,)),
            dma((nz - 1,)),
            dma((nz - 1,)),
            dma((nx * ny - 1,)),
            dma((nx * ny - 1,)),
        ],
        compiler_params=pltpu.CompilerParams(
            collective_id=0, has_side_effects=True, vmem_limit_bytes=32 * 2**20
        ),
    )(
        stay(inputs.reshape(chunks, step, features)),
        stay(weights),
        stay(cotangent.reshape(4, chunks, step, width)),
        stay(gain),
        stay(snapshot.reshape(nx * ny, size, width)),
        stay(global_rows),
        stay(momentum),
    )
    kept = [pltpu.with_memory_space_constraint(value, pltpu.VMEM) for value in kept]
    return pl.pallas_call(
        update_kernel,
        name="update",
        out_shape=(
            jax.ShapeDtypeStruct((features, width), bf16),
            jax.ShapeDtypeStruct((height, width), f32),
            jax.ShapeDtypeStruct((height, width), f32),
        ),
        in_specs=[vmem] * 8,
        out_specs=(hbm,) * 3,
        scratch_shapes=[
            pltpu.VMEM((features, width), bf16),
            pltpu.VMEM((height, width), f32),
            pltpu.VMEM((height, width), f32),
            pltpu.VMEM((height, width), bf16),
            dma((features // height,)),
            dma((3,)),
        ],
        compiler_params=pltpu.CompilerParams(vmem_limit_bytes=16 * 2**20),
    )(plan, delay, *kept)


def solution(mesh):
    in_specs = (
        P(("replica", "fsdp"), None),
        P("replica", "fsdp"),
        P("replica", "fsdp"),
        P("fsdp"),
        P("replica", "fsdp"),
        P(None, "fsdp"),
        P(None, "fsdp"),
        P(),
        P(),
    )
    out_specs = (P("replica", "fsdp"), P(None, "fsdp"), P(None, "fsdp"))
    return jax.shard_map(local, mesh=mesh, in_specs=in_specs, out_specs=out_specs, check_vma=False)
```
